32 devices in a mesh: expert: 16 (over z, y, x), dp: 2 (over core).
Axes of the slice: x: 2, y: 2, z: 4, core: 2. Of those that a mesh axis runs over, the one named last changes fastest.
Arguments:
- tokens: bfloat16 [256, 3584], P('expert', 'dp'), may hold values from -6 to 6
- expert_ids: int32 [256, 8], P('expert'), may hold values from 0 to 15, all different within a row; in each aligned block of 16 rows (0 to 15, 16 to 31, ...) at most 16 rows name the same one
- route_weight: float32 [256, 8], P('expert'), may hold values from 0.1 to 1
- swap_flags: int32 [8], replicated, may hold values from 0 to 1, as said below
- w_gate: bfloat16 [16, 1024, 3584], P('expert', None, 'dp'), may hold values from -0.09375 to 0.09375
- w_up: bfloat16 [16, 1024, 3584], P('expert', None, 'dp'), may hold values from -0.09375 to 0.09375
- w_down: bfloat16 [16, 1024, 3584], P('expert', None, 'dp'), may hold values from -0.1875 to 0.1875
- cotangent: bfloat16 [256, 3584], P('expert', 'dp'), may hold values from -0.75 to 0.75
Outputs:
- mixed: bfloat16 [256, 3584], P('expert', 'dp')
- input_grad: bfloat16 [256, 3584], P('expert', 'dp')
- grad_gate: bfloat16 [16, 1024, 3584], P('expert', None, 'dp')
- grad_up: bfloat16 [16, 1024, 3584], P('expert', None, 'dp')
- grad_down: bfloat16 [16, 1024, 3584], P('expert', None, 'dp')
The draws below stay inside these ranges and needn't reach their ends.
Inputs may be any that keep to these rules, and one draw needn't show every extreme that they name: `expert_ids`: in the 16 rows of one index of the expert axis (aligned blocks), each expert is named by at most 16 rows, a bound that some block reaches; a row names 8 different experts. `swap_flags`: entry p is 1 where slots p and p + 8 hold each other's experts; entry 0 is always 1, the others are 0 or 1.
All inputs are finite; a program needn't handle non-finite values.
Results may differ from the reference program's by a relative error of at most 0.0065.
Values may be sent and summed in bfloat16 or wider, within the bound.
A program may use at most 64 MiB of HBM per device.

```python
import math
import jax
import jax.numpy as jnp
import numpy as np
from jax import lax

D = 3584
FF = 1024
TOPK = 8
TOK_DEV = 16
EXPERTS = 16
CAP = 16
TOKENS = 256


def draw_swap_flags(key, part):
    flag_bits = jax.random.randint(key, (EXPERTS // 2,), 0, 2, dtype=jnp.int32)
    positions = jnp.arange(EXPERTS // 2, dtype=jnp.int32)
    return jnp.where(positions == 0, 1, flag_bits).astype(jnp.int32)


def levels(own_key, shape, cuts, smallest, top_value):
    def one(dim, shards_of):
        heights = jax.random.uniform(jax.random.fold_in(jax.random.fold_in(own_key, 6), dim), (shards_of,), jnp.float32, smallest / len(cuts), top_value / len(cuts))
        return jnp.repeat(jnp.exp(heights), shape[dim] // shards_of).reshape((-1,) + (1,) * (len(shape) - dim - 1))

    level = one(*cuts[0])
    for cut in cuts[1:]:
        level = level * one(*cut)
    return level


def shared_out(rng, own, number, rows, count, top, reach, lean):
    ranking = jax.random.permutation(rng, count)
    heavy_load, usual = shares(count, rows * top, reach, lean, True), shares(count, rows * top, reach, lean, False)
    places = jnp.arange(count)

    def named(sizes, offset_by):
        used = int((sizes > 0).sum())
        fixed = max(1, used // 4)
        passed = fixed + (places - fixed + offset_by * (used - fixed)) % max(1, count - fixed)
        return jnp.zeros((count,), jnp.int32).at[ranking[jnp.where(places < fixed, places, passed)]].set(jnp.asarray(sizes, jnp.int32))

    sizes = jnp.where(number % 4 == 0, named(heavy_load, number // 4), named(usual, number - number // 4 - 1))
    mixed = jax.random.permutation(jax.random.fold_in(own, 3), count)
    donor, receiver = mixed[0:count // 2 * 2:2], mixed[1:count // 2 * 2:2]
    margin = jnp.minimum(sizes[donor] - 1, reach - sizes[receiver]) // 2
    margin = jnp.where((donor == ranking[0]) | (receiver == ranking[0]) | (sizes[receiver] == 0), 0, jnp.maximum(margin, 0))
    passed = jax.random.randint(jax.random.fold_in(own, 4), (count // 2,), 0, 1 << 20) % (margin + 1)
    sizes = sizes.at[donor].add(-passed).at[receiver].add(passed)
    members = jnp.searchsorted(jnp.cumsum(sizes), jnp.arange(rows * top), side="right").astype(jnp.int32)
    table = members.reshape(top, rows).T
    table = table[jax.random.permutation(jax.random.fold_in(own, 1), rows)]
    offset_by = jax.random.randint(jax.random.fold_in(own, 2), (rows, 1), 0, top)
    return jnp.take_along_axis(table, (jnp.arange(top)[None, :] + offset_by) % top, axis=1)


def shares(amount, total, reach, lean, full):
    portions = [(1 << 20) // math.isqrt(standing ** lean) + 1 for standing in range(1, amount + 1)]
    largest = reach if full else min(reach, max(-(-total // amount), total * portions[0] // sum(portions)))
    least = 1 if total - largest >= amount - 1 else 0
    given, surplus = [largest] + [least] * (amount - 1), total - largest - least * (amount - 1)
    while surplus > 0:
        movable = [i for i in range(1, amount) if given[i] < largest] or [i for i in range(1, amount) if given[i] < reach]
        whole, remaining = sum([portions[i] for i in movable]), surplus
        for i in movable:
            extra = min(reach - given[i], max(1, remaining * portions[i] // whole), surplus)
            given[i] = given[i] + extra
            surplus = surplus - extra
    return np.array(given)


def centred(rng, extent, spread, reach, split=(), kind=jnp.bfloat16):
    drawn = spread * jax.random.normal(rng, extent, jnp.float32)
    if split:
        drawn = drawn * levels(rng, extent, split, -0.22, 0.18)
    return jnp.clip(drawn, -reach, reach).astype(kind)


def setup_inputs(seed: int = 0) -> dict:
    key_of = jax.random.split(jax.random.key(seed), 9)
    tokens = centred(key_of[0], (TOKENS, D), 1.0, 6.0, ((0, 16), (1, 2)))
    expert_ids_keys = jax.random.split(jax.random.fold_in(key_of[1], 1), TOKENS // TOK_DEV)
    expert_ids_turns = jax.random.permutation(jax.random.fold_in(key_of[1], 3), TOKENS // TOK_DEV)
    expert_ids = jax.vmap(lambda own, number: shared_out(jax.random.fold_in(key_of[1], 2), own, number, TOK_DEV, EXPERTS, TOPK, CAP, 2))(expert_ids_keys, expert_ids_turns).reshape((TOKENS, TOPK))
    route_weight = jnp.clip(0.1 + 0.9 * jax.random.uniform(key_of[2], (TOKENS, TOPK), jnp.float32) ** levels(key_of[2], (TOKENS, TOPK), ((0, 16),), -0.2, 0.2), 0.1, 1.0)
    swap_flags = draw_swap_flags(jax.random.fold_in(key_of[8], 71), 0)
    w_gate = centred(key_of[4], (EXPERTS, FF, D), D ** -0.5, 0.09375, ((0, 16), (2, 2)))
    w_up = centred(key_of[5], (EXPERTS, FF, D), D ** -0.5, 0.09375, ((0, 16), (2, 2)))
    w_down = centred(key_of[6], (EXPERTS, FF, D), FF ** -0.5, 0.1875, ((0, 16), (2, 2)))
    cotangent = centred(key_of[7], (TOKENS, D), 0.125, 0.75, ((0, 16), (1, 2)))
    return {"tokens": tokens, "expert_ids": expert_ids, "route_weight": route_weight, "swap_flags": swap_flags, "w_gate": w_gate, "w_up": w_up, "w_down": w_down, "cotangent": cotangent}


def silu_parts(pre_gate):
    sigma = jax.nn.sigmoid(pre_gate)
    return pre_gate * sigma, sigma * (1.0 + pre_gate * (1.0 - sigma))


def reference(tokens, expert_ids, route_weight, swap_flags, w_gate, w_up, w_down, cotangent):
    row_total = TOKENS * TOPK
    most_rows = CAP * EXPERTS
    flat_ids = expert_ids.reshape(row_total)
    owners = (jnp.arange(row_total, dtype=jnp.int32) // TOPK).astype(jnp.int32)
    scaled = route_weight[:, :, None] * cotangent.astype(jnp.float32)[:, None, :]
    grad_rows = scaled.reshape(row_total, D).astype(jnp.bfloat16)
    zero_row = jnp.zeros((1, D), jnp.bfloat16)
    token_pad = jnp.concatenate([tokens, zero_row], 0)
    grad_pad = jnp.concatenate([grad_rows, zero_row], 0)
    owner_pad = jnp.concatenate([owners, jnp.full((1,), TOKENS, jnp.int32)], 0).astype(jnp.int32)

    def one_expert(carry, expert):
        out_store, back_store = carry
        picked = jnp.nonzero(flat_ids == expert, size=most_rows, fill_value=row_total)[0].astype(jnp.int32)
        in_rows = token_pad[owner_pad[picked]]
        out_grads = grad_pad[picked]
        gate_w = w_gate[expert]
        up_w = w_up[expert]
        down_w = w_down[expert]
        pre_gate = jnp.dot(in_rows, gate_w.T, preferred_element_type=jnp.float32)
        up_value = jnp.dot(in_rows, up_w.T, preferred_element_type=jnp.float32)
        activated, slope = silu_parts(pre_gate)
        hidden = (activated * up_value).astype(jnp.bfloat16)
        expert_out = jnp.dot(hidden, down_w, preferred_element_type=jnp.float32).astype(jnp.bfloat16)
        hidden_grad = jnp.dot(out_grads, down_w.T, preferred_element_type=jnp.float32)
        gate_grad = (hidden_grad * up_value * slope).astype(jnp.bfloat16)
        up_grad = (hidden_grad * activated).astype(jnp.bfloat16)
        grad_g = jnp.dot(gate_grad.T, in_rows, preferred_element_type=jnp.float32).astype(jnp.bfloat16)
        grad_u = jnp.dot(up_grad.T, in_rows, preferred_element_type=jnp.float32).astype(jnp.bfloat16)
        grad_d = jnp.dot(hidden.T, out_grads, preferred_element_type=jnp.float32).astype(jnp.bfloat16)
        row_back = (jnp.dot(gate_grad, gate_w, preferred_element_type=jnp.float32)
                    + jnp.dot(up_grad, up_w, preferred_element_type=jnp.float32)).astype(jnp.bfloat16)
        out_store = out_store.at[picked].set(expert_out)
        back_store = back_store.at[picked].set(row_back)
        return (out_store, back_store), (grad_g, grad_u, grad_d)

    start_store = (jnp.zeros((row_total + 1, D), jnp.bfloat16), jnp.zeros((row_total + 1, D), jnp.bfloat16))
    (out_store, back_store), stacked = lax.scan(one_expert, start_store, jnp.arange(EXPERTS, dtype=jnp.int32))
    out_rows = out_store[:row_total].reshape(TOKENS, TOPK, D).astype(jnp.float32)
    mixed = jnp.sum(route_weight[:, :, None] * out_rows, axis=1).astype(jnp.bfloat16)
    back_rows = back_store[:row_total].reshape(TOKENS, TOPK, D).astype(jnp.float32)
    input_grad = jnp.sum(back_rows, axis=1).astype(jnp.bfloat16)
    slot_ids = jnp.arange(EXPERTS, dtype=jnp.int32)
    partner = ((slot_ids + EXPERTS // 2) % EXPERTS).astype(jnp.int32)
    resident = jnp.where(swap_flags[slot_ids % (EXPERTS // 2)] == 1, partner, slot_ids).astype(jnp.int32)
    return mixed, input_grad, stacked[0][resident], stacked[1][resident], stacked[2][resident]
```

```python
import jax
import jax.numpy as jnp
from jax import lax
from jax.sharding import PartitionSpec as P


def silu_parts(pre_gate):
    sigma = jax.nn.sigmoid(pre_gate)
    return (pre_gate * sigma, sigma * (1.0 + pre_gate * (1.0 - sigma)))


def contract_first(left_side, right_side):
    return lax.dot_general(
        left_side, right_side, (((0,), (0,)), ((), ())), preferred_element_type=jnp.float32
    )


def contract_last(left_side, right_side):
    return lax.dot_general(
        left_side, right_side, (((1,), (1,)), ((), ())), preferred_element_type=jnp.float32
    )


def per_device(tokens, expert_ids, route_weight, swap_flags, w_gate, w_up, w_down, cotangent):
    experts = lax.axis_size("expert")
    half_axis = experts // 2
    my_index = lax.axis_index("expert")
    my_flag = swap_flags[my_index % half_axis] == 1
    gate_w, up_w, down_w = w_gate[0], w_up[0], w_down[0]
    pairs = [(source, (source + half_axis) % experts) for source in range(experts)]

    chosen = lax.all_gather(expert_ids, "expert", axis=0, tiled=True) == my_index
    weights = lax.all_gather(route_weight, "expert", axis=0, tiled=True)
    in_rows = lax.all_gather(tokens, "expert", axis=0, tiled=True)
    grad_rows = lax.all_gather(cotangent, "expert", axis=0, tiled=True)
    weight = jnp.sum(jnp.where(chosen, weights, 0.0), axis=1, keepdims=True)
    picked = jnp.any(chosen, axis=1, keepdims=True)

    def share_sum(part):
        return lax.psum_scatter(part, "dp", scatter_dimension=1, tiled=True)

    def whole(share):
        return lax.all_gather(share, "dp", axis=1, tiled=True)

    pre_gate = share_sum(contract_last(in_rows, gate_w))
    up_value = share_sum(contract_last(in_rows, up_w))
    activated, slope = silu_parts(pre_gate)
    hidden = jnp.where(picked, activated * up_value, 0.0)
    weighted = (weight * hidden).astype(jnp.bfloat16)
    hidden = hidden.astype(jnp.bfloat16)
    out_part = weight * jnp.dot(whole(hidden), down_w, preferred_element_type=jnp.float32)
    mixed = lax.psum_scatter(
        out_part.astype(jnp.bfloat16), "expert", scatter_dimension=0, tiled=True
    )
    hidden_grad = weight * share_sum(contract_last(grad_rows, down_w))
    gate_grad = (hidden_grad * up_value * slope).astype(jnp.bfloat16)
    up_grad = (hidden_grad * activated).astype(jnp.bfloat16)
    back_part = jnp.dot(
        whole(gate_grad), gate_w, preferred_element_type=jnp.float32
    ) + jnp.dot(whole(up_grad), up_w, preferred_element_type=jnp.float32)
    input_grad = lax.psum_scatter(
        back_part.astype(jnp.bfloat16), "expert", scatter_dimension=0, tiled=True
    )

    def held(share):
        return whole(jnp.where(my_flag, lax.ppermute(share, "expert", pairs), share))

    grads = (
        contract_first(held(gate_grad), in_rows).astype(jnp.bfloat16),
        contract_first(held(up_grad), in_rows).astype(jnp.bfloat16),
        contract_first(held(weighted), grad_rows).astype(jnp.bfloat16),
    )
    return (mixed, input_grad, grads[0][None], grads[1][None], grads[2][None])


def solution(mesh):
    return jax.shard_map(
        per_device,
        mesh=mesh,
        in_specs=(
            P("expert", "dp"),
            P("expert", None),
            P("expert", None),
            P(),
            P("expert", None, "dp"),
            P("expert", None, "dp"),
            P("expert", None, "dp"),
            P("expert", "dp"),
        ),
        out_specs=(
            P("expert", "dp"),
            P("expert", "dp"),
            P("expert", None, "dp"),
            P("expert", None, "dp"),
            P("expert", None, "dp"),
        ),
        check_vma=False,
    )
```

```python
import jax
import jax.numpy as jnp
from jax import lax
from jax.experimental import pallas as pl
from jax.experimental.pallas import tpu as pltpu
from jax.sharding import PartitionSpec as P


def silu_parts(pre_gate):
    sigma = jax.nn.sigmoid(pre_gate)
    return (pre_gate * sigma, sigma * (1.0 + pre_gate * (1.0 - sigma)))


def contract_first(left_side, right_side):
    return lax.dot_general(
        left_side, right_side, (((0,), (0,)), ((), ())), preferred_element_type=jnp.float32
    )


def contract_last(left_side, right_side):
    return lax.dot_general(
        left_side, right_side, (((1,), (1,)), ((), ())), preferred_element_type=jnp.float32
    )


def plain_device(tokens, expert_ids, route_weight, swap_flags, w_gate, w_up, w_down, cotangent):
    experts = lax.axis_size("expert")
    half_axis = experts // 2
    my_index = lax.axis_index("expert")
    my_flag = swap_flags[my_index % half_axis] == 1
    gate_w, up_w, down_w = w_gate[0], w_up[0], w_down[0]
    pairs = [(source, (source + half_axis) % experts) for source in range(experts)]

    chosen = lax.all_gather(expert_ids, "expert", axis=0, tiled=True) == my_index
    weights = lax.all_gather(route_weight, "expert", axis=0, tiled=True)
    in_rows = lax.all_gather(tokens, "expert", axis=0, tiled=True)
    grad_rows = lax.all_gather(cotangent, "expert", axis=0, tiled=True)
    weight = jnp.sum(jnp.where(chosen, weights, 0.0), axis=1, keepdims=True)
    picked = jnp.any(chosen, axis=1, keepdims=True)

    def share_sum(part):
        return lax.psum_scatter(part, "dp", scatter_dimension=1, tiled=True)

    def whole(share):
        return lax.all_gather(share, "dp", axis=1, tiled=True)

    pre_gate = share_sum(contract_last(in_rows, gate_w))
    up_value = share_sum(contract_last(in_rows, up_w))
    activated, slope = silu_parts(pre_gate)
    hidden = jnp.where(picked, activated * up_value, 0.0)
    weighted = (weight * hidden).astype(jnp.bfloat16)
    hidden = hidden.astype(jnp.bfloat16)
    out_part = weight * jnp.dot(whole(hidden), down_w, preferred_element_type=jnp.float32)
    mixed = lax.psum_scatter(
        out_part.astype(jnp.bfloat16), "expert", scatter_dimension=0, tiled=True
    )
    hidden_grad = weight * share_sum(contract_last(grad_rows, down_w))
    gate_grad = (hidden_grad * up_value * slope).astype(jnp.bfloat16)
    up_grad = (hidden_grad * activated).astype(jnp.bfloat16)
    back_part = jnp.dot(
        whole(gate_grad), gate_w, preferred_element_type=jnp.float32
    ) + jnp.dot(whole(up_grad), up_w, preferred_element_type=jnp.float32)
    input_grad = lax.psum_scatter(
        back_part.astype(jnp.bfloat16), "expert", scatter_dimension=0, tiled=True
    )

    def held(share):
        return whole(jnp.where(my_flag, lax.ppermute(share, "expert", pairs), share))

    grads = (
        contract_first(held(gate_grad), in_rows).astype(jnp.bfloat16),
        contract_first(held(up_grad), in_rows).astype(jnp.bfloat16),
        contract_first(held(weighted), grad_rows).astype(jnp.bfloat16),
    )
    return (mixed, input_grad, grads[0][None], grads[1][None], grads[2][None])


LANES = 128
TILE = 256
ROUTES = 48


def layer_kernel(
    tokens, ids, route, flags, w_gate, w_up, w_down, cotangent,
    mixed, input_grad, rows, grads, held,
    gate_w, up_w, down_w, table, weight, total, lean, ours, theirs, outgoing, gate_by, up_by,
    whole_share, swapped, first_in, second_out, second_in, last_own, last_out, last_in,
    load_sem, send_sem, recv_sem,
):
    depth = rows.shape[0]
    tok_count, feat = tokens.shape
    count = depth * 4 * tok_count
    half = feat // 2
    share = w_gate.shape[0] // 2
    me, core = lax.axis_index("expert"), lax.axis_index("dp")
    z, y, x = me // 4, (me // 2) % 2, me % 2
    other_x, other_y, other_core = 1 - x, 1 - y, 1 - core
    low, high = pl.ds(0, half), pl.ds(half, half)

    def place(at_z, at_y, at_x):
        return {"expert": at_z * 4 + at_y * 2 + at_x}

    beside_x, beside_y, beside_core = place(z, y, other_x), place(z, other_y, x), {"dp": other_core}
    far = [place(lax.rem(z + step, depth), y, x) for step in range(1, depth)]
    opposite = place(lax.rem(z + depth // 2, depth), y, x)

    loads = []
    for number, (source, target) in enumerate(
        ((w_gate, gate_w), (w_up, up_w), (w_down, down_w))
    ):
        loads.append(pltpu.make_async_copy(source, target, load_sem.at[number]))
        loads[-1].start()

    barrier = pltpu.get_barrier_semaphore()
    peers = far + [beside_x, beside_y, beside_core]
    for peer in peers:
        pl.semaphore_signal(
            barrier, inc=1, device_id=peer, device_id_type=pl.DeviceIdType.MESH
        )
    lanes = lax.broadcasted_iota(jnp.int32, (tok_count, LANES), 1)
    entry = jnp.zeros((tok_count, LANES), jnp.float32)
    for choice in range(ids.shape[1]):
        picked = ids[:, choice : choice + 1] == lanes
        entry += jnp.where(picked, route[:, choice : choice + 1], 0.0)
    table[z, y, x] = entry
    rows[z, y, x] = tokens[...]
    grads[z, y, x] = cotangent[...]
    pl.semaphore_wait(barrier, len(peers))

    sent = []

    def push(source, target, device):
        number = len(sent)
        copy = pltpu.make_async_remote_copy(
            src_ref=source,
            dst_ref=target,
            send_sem=send_sem.at[number],
            recv_sem=recv_sem.at[number],
            device_id=device,
            device_id_type=pl.DeviceIdType.MESH,
        )
        copy.start()
        sent.append(copy)
        return copy

    def arrive(copies):
        for copy in copies:
            copy.wait_recv()

    def same(ref, device):
        return push(ref, ref, device)

    def along_z(buffer):
        return [same(buffer.at[z, y, x], peer) for peer in far]

    def spread_one(buffer):
        return (
            same(buffer.at[:, y, x, :, low], beside_x),
            same(buffer.at[:, y, x, :, high], beside_y),
        )

    def spread_two(buffer, copies):
        copies[0].wait_recv()
        onward = same(buffer.at[:, y, :, :, low], beside_y)
        copies[1].wait_recv()
        return onward, same(buffer.at[:, :, x, :, high], beside_x)

    token_z = along_z(rows)
    table_z = along_z(table)
    arrive(token_z)
    grad_z = along_z(grads)
    token_one = spread_one(rows)
    arrive(table_z)
    table_one = same(table.at[:, y, x], beside_x)
    token_two = spread_two(rows, token_one)
    table_one.wait_recv()
    table_two = same(table.at[:, y], beside_y)
    arrive(grad_z)
    grad_one = spread_one(grads)
    arrive(token_two)
    table_two.wait_recv()
    every = table[...].reshape(count, LANES)
    mine = lax.broadcasted_iota(jnp.int32, (count, LANES), 1) == me
    weight[...] = jnp.broadcast_to(
        jnp.sum(jnp.where(mine, every, 0.0), axis=1, keepdims=True), (count, LANES)
    )

    def project(buffer, matrix, first, target):
        def tile(step, carry):
            units = pl.ds(pl.multiple_of(first + step * TILE, TILE), TILE)
            columns = pl.ds(pl.multiple_of(step * TILE, TILE), TILE)
            target[:, columns] = contract_last(
                buffer[...].reshape(count, feat), matrix[units, :]
            )
            return carry

        lax.fori_loop(0, share // TILE, tile, 0)

    def partial(number, buffer, matrix):
        project(buffer, matrix, other_core * share, outgoing.at[number])
        return push(outgoing.at[number], theirs.at[number], beside_core)

    loads[0].wait()
    gate_sum = partial(0, rows, gate_w)
    loads[1].wait()
    up_sum = partial(1, rows, up_w)
    project(rows, gate_w, core * share, ours.at[0])
    grad_two = spread_two(grads, grad_one)
    project(rows, up_w, core * share, ours.at[1])
    loads[2].wait()
    arrive((gate_sum, up_sum))

    chunk = 2 * tok_count

    def activate(step, carry):
        part = pl.ds(pl.multiple_of(step * chunk, chunk), chunk)
        scale = weight[part, 0:1]
        up_value = ours[1, part, :] + theirs[1, part, :]
        activated, slope = silu_parts(ours[0, part, :] + theirs[0, part, :])
        hidden = activated * up_value
        whole_share[0, core, part, :] = hidden.astype(jnp.bfloat16)
        swapped[0, part, :] = (scale * hidden).astype(jnp.bfloat16)
        gate_by[part, :] = scale * up_value * slope
        up_by[part, :] = scale * activated
        return carry

    lax.fori_loop(0, count // chunk, activate, 0)
    hidden_share = same(whole_share.at[0, core], beside_core)
    trades = [push(swapped.at[0], swapped.at[1], opposite)]
    hidden_share.wait_recv()

    def combine(number, terms, scaled):
        def tile(step, carry):
            columns = pl.ds(pl.multiple_of(step * TILE, TILE), TILE)
            result = jnp.zeros((count, TILE), jnp.float32)
            for source, matrix in terms:
                for side in range(2):
                    result += jnp.dot(
                        whole_share[source, side],
                        matrix[side * share : (side + 1) * share, columns],
                        preferred_element_type=jnp.float32,
                    )
            if scaled:
                result = result * weight[:, 0:1]
            result = result.reshape(depth, 2, 2, tok_count, TILE)
            total[number, :, :, :, :, columns] = result
            lean[number, :, :, :, :, columns] = result.astype(jnp.bfloat16)
            return carry

        lax.fori_loop(0, feat // TILE, tile, 0)

    def reduce_one(number):
        return (
            push(lean.at[number, :, other_y, :, :, low], first_in.at[number, 0], beside_y),
            push(lean.at[number, :, :, other_x, :, high], first_in.at[number, 1], beside_x),
        )

    def reduce_two(number, copies):
        copies[0].wait_recv()
        second_out[number, 0] = (
            total[number, :, y, other_x, :, low]
            + first_in[number, 0, :, other_x].astype(jnp.float32)
        ).astype(jnp.bfloat16)
        onward = push(second_out.at[number, 0], second_in.at[number, 0], beside_x)
        copies[1].wait_recv()
        second_out[number, 1] = (
            total[number, :, other_y, x, :, high]
            + first_in[number, 1, :, other_y].astype(jnp.float32)
        ).astype(jnp.bfloat16)
        return onward, push(second_out.at[number, 1], second_in.at[number, 1], beside_y)

    def reduce_three(number, copies):
        arrive(copies)
        for side, (columns, index) in enumerate(((low, x), (high, y))):
            result = (
                total[number, :, y, x, :, columns]
                + first_in[number, side, :, index].astype(jnp.float32)
                + second_in[number, side].astype(jnp.float32)
            )
            last_own[number, :, :, columns] = result
            last_out[number, :, :, columns] = result.astype(jnp.bfloat16)
        return [
            push(
                last_out.at[number, lax.rem(z + step, depth)],
                last_in.at[number, step - 1],
                far[step - 1],
            )
            for step in range(1, depth)
        ]

    def reduce_end(number, copies, target):
        arrive(copies)
        result = last_own[number, z]
        for step in range(depth - 1):
            result += last_in[number, step].astype(jnp.float32)
        target[...] = result.astype(jnp.bfloat16)

    combine(0, ((0, down_w),), True)
    mixed_one = reduce_one(0)
    arrive(grad_two)
    grad_sum = partial(2, grads, down_w)
    project(grads, down_w, core * share, ours.at[2])
    grad_sum.wait_recv()

    def backward(step, carry):
        part = pl.ds(pl.multiple_of(step * chunk, chunk), chunk)
        hidden_grad = ours[2, part, :] + theirs[2, part, :]
        whole_share[1, core, part, :] = (hidden_grad * gate_by[part, :]).astype(jnp.bfloat16)
        whole_share[2, core, part, :] = (hidden_grad * up_by[part, :]).astype(jnp.bfloat16)
        return carry

    lax.fori_loop(0, count // chunk, backward, 0)
    gate_share = same(whole_share.at[1, core], beside_core)
    up_share = same(whole_share.at[2, core], beside_core)
    trades.append(push(whole_share.at[1, core], swapped.at[2], opposite))
    trades.append(push(whole_share.at[2, core], swapped.at[3], opposite))
    mixed_two = reduce_two(0, mixed_one)
    arrive((gate_share, up_share))
    combine(1, ((1, gate_w), (2, up_w)), False)
    back_one = reduce_one(1)
    mixed_three = reduce_three(0, mixed_two)
    back_two = reduce_two(1, back_one)
    back_three = reduce_three(1, back_two)

    flag = flags[0, me % (2 * depth)] == 1
    kept = []
    for number in range(3):
        trades[number].wait_recv()
        own = swapped[0] if number == 0 else whole_share[number, core]
        held[number, core] = jnp.where(flag, swapped[number + 1], own)
        kept.append(same(held.at[number, core], beside_core))
    reduce_end(0, mixed_three, mixed)
    reduce_end(1, back_three, input_grad)
    arrive(kept)
    for copy in sent:
        copy.wait_send()


def kernel_device(tokens, expert_ids, route_weight, swap_flags, w_gate, w_up, w_down, cotangent):
    tok_count, feat = tokens.shape
    depth = lax.axis_size("expert") // 4
    count = depth * 4 * tok_count
    units = w_gate.shape[1]
    share = units // 2
    half = feat // 2
    narrow, wide = jnp.bfloat16, jnp.float32
    grid = (depth, 2, 2, tok_count)
    vmem = pl.BlockSpec(memory_space=pltpu.VMEM)
    smem = pl.BlockSpec(memory_space=pltpu.SMEM)
    hbm = pl.BlockSpec(memory_space=pl.ANY)
    mixed, input_grad, rows, grads, held = pl.pallas_call(
        layer_kernel,
        out_shape=(
            jax.ShapeDtypeStruct((tok_count, feat), narrow),
            jax.ShapeDtypeStruct((tok_count, feat), narrow),
            jax.ShapeDtypeStruct(grid + (feat,), narrow),
            jax.ShapeDtypeStruct(grid + (feat,), narrow),
            jax.ShapeDtypeStruct((3, 2, count, share), narrow),
        ),
        in_specs=[vmem, vmem, vmem, smem, hbm, hbm, hbm, vmem],
        out_specs=(vmem,) * 5,
        scratch_shapes=[
            pltpu.VMEM((units, feat), narrow),
            pltpu.VMEM((units, feat), narrow),
            pltpu.VMEM((units, feat), narrow),
            pltpu.VMEM(grid + (LANES,), wide),
            pltpu.VMEM((count, LANES), wide),
            pltpu.VMEM((2,) + grid + (feat,), wide),
            pltpu.VMEM((2,) + grid + (feat,), narrow),
            pltpu.VMEM((3, count, share), wide),
            pltpu.VMEM((3, count, share), wide),
            pltpu.VMEM((3, count, share), wide),
            pltpu.VMEM((count, share), wide),
            pltpu.VMEM((count, share), wide),
            pltpu.VMEM((3, 2, count, share), narrow),
            pltpu.VMEM((4, count, share), narrow),
            pltpu.VMEM((2, 2, depth, 2, tok_count, half), narrow),
            pltpu.VMEM((2, 2, depth, tok_count, half), narrow),
            pltpu.VMEM((2, 2, depth, tok_count, half), narrow),
            pltpu.VMEM((2, depth, tok_count, feat), wide),
            pltpu.VMEM((2, depth, tok_count, feat), narrow),
            pltpu.VMEM((2, depth - 1, tok_count, feat), narrow),
            pltpu.SemaphoreType.DMA((3,)),
            pltpu.SemaphoreType.DMA((ROUTES,)),
            pltpu.SemaphoreType.DMA((ROUTES,)),
        ],
        compiler_params=pltpu.CompilerParams(
            collective_id=0, has_side_effects=True, vmem_limit_bytes=56 * 2**20
        ),
    )(
        tokens, expert_ids, route_weight, swap_flags[None], w_gate[0], w_up[0], w_down[0],
        cotangent,
    )
    rows, grads = rows.reshape(count, feat), grads.reshape(count, feat)

    def outer(operand, other):
        product = lax.dot_general(
            operand, other, (((1,), (0,)), ((), ())), preferred_element_type=jnp.float32
        )
        return product.astype(narrow).reshape(1, units, feat)

    return mixed, input_grad, outer(held[1], rows), outer(held[2], rows), outer(held[0], grads)


def per_device(*operands):
    experts, shards = lax.axis_size("expert"), lax.axis_size("dp")
    tok_count, feat = operands[0].shape
    units = operands[4].shape[1]
    fits = 8 <= experts <= 16 and experts % 8 == 0 and shards == 2 and tok_count % 16 == 0
    fits = fits and feat % TILE == 0 and units % (2 * TILE) == 0
    fits = fits and 3 * units * feat <= 6 * 2**20 and experts * tok_count <= 256
    return kernel_device(*operands) if fits else plain_device(*operands)


def solution(mesh):
    return jax.shard_map(
        per_device,
        mesh=mesh,
        in_specs=(
            P("expert", "dp"),
            P("expert", None),
            P("expert", None),
            P(),
            P("expert", None, "dp"),
            P("expert", None, "dp"),
            P("expert", None, "dp"),
            P("expert", "dp"),
        ),
        out_specs=(
            P("expert", "dp"),
            P("expert", "dp"),
            P("expert", None, "dp"),
            P("expert", None, "dp"),
            P("expert", None, "dp"),
        ),
        check_vma=False,
    )
```

```python
import jax
import jax.numpy as jnp
from jax import lax
from jax.experimental import pallas as pl
from jax.experimental.pallas import tpu as pltpu
from jax.sharding import PartitionSpec as P


def silu_parts(pre_gate):
    sigma = jax.nn.sigmoid(pre_gate)
    return (pre_gate * sigma, sigma * (1.0 + pre_gate * (1.0 - sigma)))


def contract_first(left_side, right_side):
    return lax.dot_general(
        left_side, right_side, (((0,), (0,)), ((), ())), preferred_element_type=jnp.float32
    )


def contract_last(left_side, right_side):
    return lax.dot_general(
        left_side, right_side, (((1,), (1,)), ((), ())), preferred_element_type=jnp.float32
    )


def plain_device(tokens, expert_ids, route_weight, swap_flags, w_gate, w_up, w_down, cotangent):
    experts = lax.axis_size("expert")
    half_axis = experts // 2
    my_index = lax.axis_index("expert")
    my_flag = swap_flags[my_index % half_axis] == 1
    gate_w, up_w, down_w = w_gate[0], w_up[0], w_down[0]
    pairs = [(source, (source + half_axis) % experts) for source in range(experts)]

    chosen = lax.all_gather(expert_ids, "expert", axis=0, tiled=True) == my_index
    weights = lax.all_gather(route_weight, "expert", axis=0, tiled=True)
    in_rows = lax.all_gather(tokens, "expert", axis=0, tiled=True)
    grad_rows = lax.all_gather(cotangent, "expert", axis=0, tiled=True)
    weight = jnp.sum(jnp.where(chosen, weights, 0.0), axis=1, keepdims=True)
    picked = jnp.any(chosen, axis=1, keepdims=True)

    def share_sum(part):
        return lax.psum_scatter(part, "dp", scatter_dimension=1, tiled=True)

    def whole(share):
        return lax.all_gather(share, "dp", axis=1, tiled=True)

    pre_gate = share_sum(contract_last(in_rows, gate_w))
    up_value = share_sum(contract_last(in_rows, up_w))
    activated, slope = silu_parts(pre_gate)
    hidden = jnp.where(picked, activated * up_value, 0.0)
    weighted = (weight * hidden).astype(jnp.bfloat16)
    hidden = hidden.astype(jnp.bfloat16)
    out_part = weight * jnp.dot(whole(hidden), down_w, preferred_element_type=jnp.float32)
    mixed = lax.psum_scatter(
        out_part.astype(jnp.bfloat16), "expert", scatter_dimension=0, tiled=True
    )
    hidden_grad = weight * share_sum(contract_last(grad_rows, down_w))
    gate_grad = (hidden_grad * up_value * slope).astype(jnp.bfloat16)
    up_grad = (hidden_grad * activated).astype(jnp.bfloat16)
    back_part = jnp.dot(
        whole(gate_grad), gate_w, preferred_element_type=jnp.float32
    ) + jnp.dot(whole(up_grad), up_w, preferred_element_type=jnp.float32)
    input_grad = lax.psum_scatter(
        back_part.astype(jnp.bfloat16), "expert", scatter_dimension=0, tiled=True
    )

    def held(share):
        return whole(jnp.where(my_flag, lax.ppermute(share, "expert", pairs), share))

    grads = (
        contract_first(held(gate_grad), in_rows).astype(jnp.bfloat16),
        contract_first(held(up_grad), in_rows).astype(jnp.bfloat16),
        contract_first(held(weighted), grad_rows).astype(jnp.bfloat16),
    )
    return (mixed, input_grad, grads[0][None], grads[1][None], grads[2][None])


LANES = 128
TILE = 256
ROUTES = 48


def layer_kernel(
    tokens, ids, route, flags, w_gate, w_up, w_down, cotangent,
    mixed, input_grad, rows, grads, held,
    gate_w, up_w, down_w, table, weight, total, lean, ours, theirs, outgoing, gate_by, up_by,
    whole_share, swapped, first_in, second_out, second_in, last_own, last_out, last_in,
    load_sem, send_sem, recv_sem,
):
    depth = rows.shape[0]
    tok_count, feat = tokens.shape
    count = depth * 4 * tok_count
    half = feat // 2
    share = w_gate.shape[0] // 2
    me, core = lax.axis_index("expert"), lax.axis_index("dp")
    z, y, x = me // 4, (me // 2) % 2, me % 2
    other_x, other_y, other_core = 1 - x, 1 - y, 1 - core
    low, high = pl.ds(0, half), pl.ds(half, half)

    def place(at_z, at_y, at_x):
        return {"expert": at_z * 4 + at_y * 2 + at_x}

    beside_x, beside_y, beside_core = place(z, y, other_x), place(z, other_y, x), {"dp": other_core}
    far = [place(lax.rem(z + step, depth), y, x) for step in range(1, depth)]
    opposite = place(lax.rem(z + depth // 2, depth), y, x)

    loads = []
    for number, (source, target) in enumerate(
        ((w_gate, gate_w), (w_up, up_w), (w_down, down_w))
    ):
        loads.append(pltpu.make_async_copy(source, target, load_sem.at[number]))
        loads[-1].start()

    barrier = pltpu.get_barrier_semaphore()
    peers = far + [beside_x, beside_y, beside_core]
    for peer in peers:
        pl.semaphore_signal(
            barrier, inc=1, device_id=peer, device_id_type=pl.DeviceIdType.MESH
        )
    experts = lax.broadcasted_iota(jnp.int32, (LANES, tok_count), 0)
    entry = jnp.zeros((LANES, tok_count), jnp.float32)
    for choice in range(ids.shape[0]):
        picked = ids[choice : choice + 1, :] == experts
        entry += jnp.where(picked, route[choice : choice + 1, :], 0.0)
    token = lax.broadcasted_iota(jnp.int32, (tok_count, tok_count), 0)
    unit = token == lax.broadcasted_iota(jnp.int32, (tok_count, tok_count), 1)
    table[z, y, x] = lax.dot_general(
        unit.astype(jnp.float32), entry, (((1,), (1,)), ((), ())),
        precision=lax.Precision.HIGHEST, preferred_element_type=jnp.float32,
    )
    rows[z, y, x] = tokens[...]
    grads[z, y, x] = cotangent[...]
    pl.semaphore_wait(barrier, len(peers))

    sent = []

    def push(source, target, device):
        number = len(sent)
        copy = pltpu.make_async_remote_copy(
            src_ref=source,
            dst_ref=target,
            send_sem=send_sem.at[number],
            recv_sem=recv_sem.at[number],
            device_id=device,
            device_id_type=pl.DeviceIdType.MESH,
        )
        copy.start()
        sent.append(copy)
        return copy

    def arrive(copies):
        for copy in copies:
            copy.wait_recv()

    def same(ref, device):
        return push(ref, ref, device)

    def along_z(buffer):
        return [same(buffer.at[z, y, x], peer) for peer in far]

    def spread_one(buffer):
        return (
            same(buffer.at[:, y, x, :, low], beside_x),
            same(buffer.at[:, y, x, :, high], beside_y),
        )

    def spread_two(buffer, copies):
        copies[0].wait_recv()
        onward = same(buffer.at[:, y, :, :, low], beside_y)
        copies[1].wait_recv()
        return onward, same(buffer.at[:, :, x, :, high], beside_x)

    token_z = along_z(rows)
    table_z = along_z(table)
    arrive(token_z)
    grad_z = along_z(grads)
    token_one = spread_one(rows)
    arrive(table_z)
    table_one = same(table.at[:, y, x], beside_x)
    token_two = spread_two(rows, token_one)
    table_one.wait_recv()
    table_two = same(table.at[:, y], beside_y)
    arrive(grad_z)
    grad_one = spread_one(grads)
    arrive(token_two)
    table_two.wait_recv()
    every = table[...].reshape(count, LANES)
    mine = lax.broadcasted_iota(jnp.int32, (count, LANES), 1) == me
    weight[...] = jnp.broadcast_to(
        jnp.sum(jnp.where(mine, every, 0.0), axis=1, keepdims=True), (count, LANES)
    )

    def project(buffer, matrix, first, target):
        def tile(step, carry):
            units = pl.ds(pl.multiple_of(first + step * TILE, TILE), TILE)
            columns = pl.ds(pl.multiple_of(step * TILE, TILE), TILE)
            target[:, columns] = contract_last(
                buffer[...].reshape(count, feat), matrix[units, :]
            )
            return carry

        lax.fori_loop(0, share // TILE, tile, 0)

    def partial(number, buffer, matrix):
        project(buffer, matrix, other_core * share, outgoing.at[number])
        return push(outgoing.at[number], theirs.at[number], beside_core)

    loads[0].wait()
    gate_sum = partial(0, rows, gate_w)
    loads[1].wait()
    up_sum = partial(1, rows, up_w)
    project(rows, gate_w, core * share, ours.at[0])
    grad_two = spread_two(grads, grad_one)
    project(rows, up_w, core * share, ours.at[1])
    loads[2].wait()
    arrive((gate_sum, up_sum))

    chunk = 2 * tok_count

    def activate(step, carry):
        part = pl.ds(pl.multiple_of(step * chunk, chunk), chunk)
        scale = weight[part, 0:1]
        up_value = ours[1, part, :] + theirs[1, part, :]
        activated, slope = silu_parts(ours[0, part, :] + theirs[0, part, :])
        hidden = activated * up_value
        whole_share[0, core, part, :] = hidden.astype(jnp.bfloat16)
        swapped[0, part, :] = (scale * hidden).astype(jnp.bfloat16)
        gate_by[part, :] = scale * up_value * slope
        up_by[part, :] = scale * activated
        return carry

    lax.fori_loop(0, count // chunk, activate, 0)
    hidden_share = same(whole_share.at[0, core], beside_core)
    trades = [push(swapped.at[0], swapped.at[1], opposite)]

    def combine(number, terms, scaled):
        def tile(step, carry):
            columns = pl.ds(pl.multiple_of(step * TILE, TILE), TILE)
            result = jnp.zeros((count, TILE), jnp.float32)
            for source, matrix in terms:
                for side in range(2):
                    result += jnp.dot(
                        whole_share[source, side],
                        matrix[side * share : (side + 1) * share, columns],
                        preferred_element_type=jnp.float32,
                    )
            if scaled:
                result = result * weight[:, 0:1]
            result = result.reshape(depth, 2, 2, tok_count, TILE)
            total[number, :, :, :, :, columns] = result
            lean[number, :, :, :, :, columns] = result.astype(jnp.bfloat16)
            return carry

        lax.fori_loop(0, feat // TILE, tile, 0)

    def reduce_one(number):
        return (
            push(lean.at[number, :, other_y, :, :, low], first_in.at[number, 0], beside_y),
            push(lean.at[number, :, :, other_x, :, high], first_in.at[number, 1], beside_x),
        )

    def reduce_two(number, copies):
        copies[0].wait_recv()
        second_out[number, 0] = (
            total[number, :, y, other_x, :, low]
            + first_in[number, 0, :, other_x].astype(jnp.float32)
        ).astype(jnp.bfloat16)
        onward = push(second_out.at[number, 0], second_in.at[number, 0], beside_x)
        copies[1].wait_recv()
        second_out[number, 1] = (
            total[number, :, other_y, x, :, high]
            + first_in[number, 1, :, other_y].astype(jnp.float32)
        ).astype(jnp.bfloat16)
        return onward, push(second_out.at[number, 1], second_in.at[number, 1], beside_y)

    def reduce_three(number, copies):
        arrive(copies)
        for side, (columns, index) in enumerate(((low, x), (high, y))):
            result = (
                total[number, :, y, x, :, columns]
                + first_in[number, side, :, index].astype(jnp.float32)
                + second_in[number, side].astype(jnp.float32)
            )
            last_own[number, :, :, columns] = result
            last_out[number, :, :, columns] = result.astype(jnp.bfloat16)
        return [
            push(
                last_out.at[number, lax.rem(z + step, depth)],
                last_in.at[number, step - 1],
                far[step - 1],
            )
            for step in range(1, depth)
        ]

    def reduce_end(number, copies, target):
        arrive(copies)
        result = last_own[number, z]
        for step in range(depth - 1):
            result += last_in[number, step].astype(jnp.float32)
        target[...] = result.astype(jnp.bfloat16)

    arrive(grad_two)
    grad_sum = partial(2, grads, down_w)
    project(grads, down_w, core * share, ours.at[2])
    grad_sum.wait_recv()

    def backward(step, carry):
        part = pl.ds(pl.multiple_of(step * chunk, chunk), chunk)
        hidden_grad = ours[2, part, :] + theirs[2, part, :]
        whole_share[1, core, part, :] = (hidden_grad * gate_by[part, :]).astype(jnp.bfloat16)
        whole_share[2, core, part, :] = (hidden_grad * up_by[part, :]).astype(jnp.bfloat16)
        return carry

    lax.fori_loop(0, count // chunk, backward, 0)
    gate_share = same(whole_share.at[1, core], beside_core)
    up_share = same(whole_share.at[2, core], beside_core)
    trades.append(push(whole_share.at[1, core], swapped.at[2], opposite))
    trades.append(push(whole_share.at[2, core], swapped.at[3], opposite))
    hidden_share.wait_recv()
    combine(0, ((0, down_w),), True)
    mixed_one = reduce_one(0)
    arrive((gate_share, up_share))
    combine(1, ((1, gate_w), (2, up_w)), False)
    back_one = reduce_one(1)
    mixed_two = reduce_two(0, mixed_one)
    mixed_three = reduce_three(0, mixed_two)
    back_two = reduce_two(1, back_one)
    back_three = reduce_three(1, back_two)

    flag = flags[0, me % (2 * depth)] == 1
    kept = []
    for number in range(3):
        trades[number].wait_recv()
        own = swapped[0] if number == 0 else whole_share[number, core]
        held[number, core] = jnp.where(flag, swapped[number + 1], own)
        kept.append(same(held.at[number, core], beside_core))
    reduce_end(0, mixed_three, mixed)
    reduce_end(1, back_three, input_grad)
    arrive(kept)
    for copy in sent:
        copy.wait_send()


def kernel_device(tokens, expert_ids, route_weight, swap_flags, w_gate, w_up, w_down, cotangent):
    tok_count, feat = tokens.shape
    depth = lax.axis_size("expert") // 4
    count = depth * 4 * tok_count
    units = w_gate.shape[1]
    share = units // 2
    half = feat // 2
    narrow, wide = jnp.bfloat16, jnp.float32
    grid = (depth, 2, 2, tok_count)
    vmem = pl.BlockSpec(memory_space=pltpu.VMEM)
    smem = pl.BlockSpec(memory_space=pltpu.SMEM)
    hbm = pl.BlockSpec(memory_space=pl.ANY)
    mixed, input_grad, rows, grads, held = pl.pallas_call(
        layer_kernel,
        out_shape=(
            jax.ShapeDtypeStruct((tok_count, feat), narrow),
            jax.ShapeDtypeStruct((tok_count, feat), narrow),
            jax.ShapeDtypeStruct(grid + (feat,), narrow),
            jax.ShapeDtypeStruct(grid + (feat,), narrow),
            jax.ShapeDtypeStruct((3, 2, count, share), narrow),
        ),
        in_specs=[vmem, vmem, vmem, smem, hbm, hbm, hbm, vmem],
        out_specs=(vmem,) * 5,
        scratch_shapes=[
            pltpu.VMEM((units, feat), narrow),
            pltpu.VMEM((units, feat), narrow),
            pltpu.VMEM((units, feat), narrow),
            pltpu.VMEM(grid + (LANES,), wide),
            pltpu.VMEM((count, LANES), wide),
            pltpu.VMEM((2,) + grid + (feat,), wide),
            pltpu.VMEM((2,) + grid + (feat,), narrow),
            pltpu.VMEM((3, count, share), wide),
            pltpu.VMEM((3, count, share), wide),
            pltpu.VMEM((3, count, share), wide),
            pltpu.VMEM((count, share), wide),
            pltpu.VMEM((count, share), wide),
            pltpu.VMEM((3, 2, count, share), narrow),
            pltpu.VMEM((4, count, share), narrow),
            pltpu.VMEM((2, 2, depth, 2, tok_count, half), narrow),
            pltpu.VMEM((2, 2, depth, tok_count, half), narrow),
            pltpu.VMEM((2, 2, depth, tok_count, half), narrow),
            pltpu.VMEM((2, depth, tok_count, feat), wide),
            pltpu.VMEM((2, depth, tok_count, feat), narrow),
            pltpu.VMEM((2, depth - 1, tok_count, feat), narrow),
            pltpu.SemaphoreType.DMA((3,)),
            pltpu.SemaphoreType.DMA((ROUTES,)),
            pltpu.SemaphoreType.DMA((ROUTES,)),
        ],
        compiler_params=pltpu.CompilerParams(
            collective_id=0, has_side_effects=True, vmem_limit_bytes=56 * 2**20
        ),
    )(
        tokens, expert_ids.T, route_weight.T, swap_flags[None], w_gate[0], w_up[0], w_down[0],
        cotangent,
    )
    rows, grads = rows.reshape(count, feat), grads.reshape(count, feat)
    tile = min(TILE, share)
    tiles = share // tile
    whole_rows = pl.BlockSpec((count, feat), lambda step: (0, 0))
    block = pl.BlockSpec((1, tile, feat), lambda step: (0, step, 0))
    gate, up, down = pl.pallas_call(
        outer_kernel,
        grid=(2 * tiles,),
        out_shape=(jax.ShapeDtypeStruct((1, units, feat), narrow),) * 3,
        in_specs=[
            pl.BlockSpec(
                (3, 1, count, tile), lambda step: (0, step // tiles, 0, lax.rem(step, tiles))
            ),
            whole_rows,
            whole_rows,
        ],
        out_specs=(block,) * 3,
        compiler_params=pltpu.CompilerParams(vmem_limit_bytes=56 * 2**20),
        cost_estimate=pl.CostEstimate(
            flops=6 * count * units * feat,
            bytes_accessed=6 * units * (feat + count) + 4 * count * feat,
            transcendentals=0,
        ),
    )(held, rows, grads)
    return mixed, input_grad, gate, up, down


def outer_kernel(held, rows, grads, gate, up, down):
    for number, other, target in ((1, rows, gate), (2, rows, up), (0, grads, down)):
        target[0] = contract_first(held[number, 0], other[...]).astype(jnp.bfloat16)


def per_device(*operands):
    experts, shards = lax.axis_size("expert"), lax.axis_size("dp")
    tok_count, feat = operands[0].shape
    units = operands[4].shape[1]
    fits = 8 <= experts <= 16 and experts % 8 == 0 and shards == 2 and tok_count % 16 == 0
    fits = fits and feat % TILE == 0 and units % (2 * TILE) == 0
    fits = fits and 3 * units * feat <= 6 * 2**20 and experts * tok_count <= 256
    return kernel_device(*operands) if fits else plain_device(*operands)


def solution(mesh):
    return jax.shard_map(
        per_device,
        mesh=mesh,
        in_specs=(
            P("expert", "dp"),
            P("expert", None),
            P("expert", None),
            P(),
            P("expert", None, "dp"),
            P("expert", None, "dp"),
            P("expert", None, "dp"),
            P("expert", "dp"),
        ),
        out_specs=(
            P("expert", "dp"),
            P("expert", "dp"),
            P("expert", None, "dp"),
            P("expert", None, "dp"),
            P("expert", None, "dp"),
        ),
        check_vma=False,
    )
```

```python
import jax
import jax.numpy as jnp
from jax import lax
from jax.experimental import pallas as pl
from jax.experimental.pallas import tpu as pltpu
from jax.sharding import PartitionSpec as P


def silu_parts(pre_gate):
    sigma = jax.nn.sigmoid(pre_gate)
    return (pre_gate * sigma, sigma * (1.0 + pre_gate * (1.0 - sigma)))


def contract_first(left_side, right_side):
    return lax.dot_general(
        left_side, right_side, (((0,), (0,)), ((), ())), preferred_element_type=jnp.float32
    )


def contract_last(left_side, right_side):
    return lax.dot_general(
        left_side, right_side, (((1,), (1,)), ((), ())), preferred_element_type=jnp.float32
    )


def plain_device(tokens, expert_ids, route_weight, swap_flags, w_gate, w_up, w_down, cotangent):
    experts = lax.axis_size("expert")
    half_axis = experts // 2
    my_index = lax.axis_index("expert")
    my_flag = swap_flags[my_index % half_axis] == 1
    gate_w, up_w, down_w = w_gate[0], w_up[0], w_down[0]
    pairs = [(source, (source + half_axis) % experts) for source in range(experts)]

    chosen = lax.all_gather(expert_ids, "expert", axis=0, tiled=True) == my_index
    weights = lax.all_gather(route_weight, "expert", axis=0, tiled=True)
    in_rows = lax.all_gather(tokens, "expert", axis=0, tiled=True)
    grad_rows = lax.all_gather(cotangent, "expert", axis=0, tiled=True)
    weight = jnp.sum(jnp.where(chosen, weights, 0.0), axis=1, keepdims=True)
    picked = jnp.any(chosen, axis=1, keepdims=True)

    def share_sum(part):
        return lax.psum_scatter(part, "dp", scatter_dimension=1, tiled=True)

    def whole(share):
        return lax.all_gather(share, "dp", axis=1, tiled=True)

    pre_gate = share_sum(contract_last(in_rows, gate_w))
    up_value = share_sum(contract_last(in_rows, up_w))
    activated, slope = silu_parts(pre_gate)
    hidden = jnp.where(picked, activated * up_value, 0.0)
    weighted = (weight * hidden).astype(jnp.bfloat16)
    hidden = hidden.astype(jnp.bfloat16)
    out_part = weight * jnp.dot(whole(hidden), down_w, preferred_element_type=jnp.float32)
    mixed = lax.psum_scatter(
        out_part.astype(jnp.bfloat16), "expert", scatter_dimension=0, tiled=True
    )
    hidden_grad = weight * share_sum(contract_last(grad_rows, down_w))
    gate_grad = (hidden_grad * up_value * slope).astype(jnp.bfloat16)
    up_grad = (hidden_grad * activated).astype(jnp.bfloat16)
    back_part = jnp.dot(
        whole(gate_grad), gate_w, preferred_element_type=jnp.float32
    ) + jnp.dot(whole(up_grad), up_w, preferred_element_type=jnp.float32)
    input_grad = lax.psum_scatter(
        back_part.astype(jnp.bfloat16), "expert", scatter_dimension=0, tiled=True
    )

    def held(share):
        return whole(jnp.where(my_flag, lax.ppermute(share, "expert", pairs), share))

    grads = (
        contract_first(held(gate_grad), in_rows).astype(jnp.bfloat16),
        contract_first(held(up_grad), in_rows).astype(jnp.bfloat16),
        contract_first(held(weighted), grad_rows).astype(jnp.bfloat16),
    )
    return (mixed, input_grad, grads[0][None], grads[1][None], grads[2][None])


LANES = 128
TILE = 256
ROUTES = 96


def layer_kernel(
    tokens, ids, route, flags, w_gate, w_up, w_down, cotangent,
    mixed, input_grad, rows, grads, held,
    gate_w, up_w, down_w, table, weight, total, lean, ours, theirs, outgoing, gate_by, up_by,
    whole_share, swapped, first_in, second_out, second_in, last_own, last_out, last_in,
    load_sem, send_sem, recv_sem,
):
    depth = rows.shape[0]
    tok_count, feat = tokens.shape
    count = depth * 4 * tok_count
    half = feat // 2
    share = w_gate.shape[0] // 2
    me, core = lax.axis_index("expert"), lax.axis_index("dp")
    z, y, x = me // 4, (me // 2) % 2, me % 2
    other_x, other_y, other_core = 1 - x, 1 - y, 1 - core
    low, high = pl.ds(0, half), pl.ds(half, half)

    def place(at_z, at_y, at_x):
        return {"expert": at_z * 4 + at_y * 2 + at_x}

    beside_x, beside_y, beside_core = place(z, y, other_x), place(z, other_y, x), {"dp": other_core}
    far = [place(lax.rem(z + step, depth), y, x) for step in range(1, depth)]
    opposite = place(lax.rem(z + depth // 2, depth), y, x)

    loads = []
    for number, (source, target) in enumerate(
        ((w_gate, gate_w), (w_up, up_w), (w_down, down_w))
    ):
        loads.append(pltpu.make_async_copy(source, target, load_sem.at[number]))
        loads[-1].start()

    barrier = pltpu.get_barrier_semaphore()
    peers = far + [beside_x, beside_y, beside_core]
    for peer in peers:
        pl.semaphore_signal(
            barrier, inc=1, device_id=peer, device_id_type=pl.DeviceIdType.MESH
        )
    experts = lax.broadcasted_iota(jnp.int32, (LANES, tok_count), 0)
    entry = jnp.zeros((LANES, tok_count), jnp.float32)
    for choice in range(ids.shape[0]):
        picked = ids[choice : choice + 1, :] == experts
        entry += jnp.where(picked, route[choice : choice + 1, :], 0.0)
    token = lax.broadcasted_iota(jnp.int32, (tok_count, tok_count), 0)
    unit = token == lax.broadcasted_iota(jnp.int32, (tok_count, tok_count), 1)
    table[z, y, x] = lax.dot_general(
        unit.astype(jnp.float32), entry, (((1,), (1,)), ((), ())),
        precision=lax.Precision.HIGHEST, preferred_element_type=jnp.float32,
    )
    rows[z, y, x] = tokens[...]
    grads[z, y, x] = cotangent[...]
    pl.semaphore_wait(barrier, len(peers))

    sent = []

    def push(source, target, device):
        number = len(sent)
        copy = pltpu.make_async_remote_copy(
            src_ref=source,
            dst_ref=target,
            send_sem=send_sem.at[number],
            recv_sem=recv_sem.at[number],
            device_id=device,
            device_id_type=pl.DeviceIdType.MESH,
        )
        copy.start()
        sent.append(copy)
        return copy

    def arrive(copies):
        for copy in copies:
            copy.wait_recv()

    def same(ref, device):
        return push(ref, ref, device)

    def along_z(buffer):
        return [same(buffer.at[z, y, x], peer) for peer in far]

    def spread_one(buffer, arriving):
        copies = []
        for step in range(depth):
            if step:
                arriving[step - 1].wait_recv()
            at_z = lax.rem(z - step + depth, depth)
            by_x = same(buffer.at[at_z, y, x, :, low], beside_x)
            by_y = same(buffer.at[at_z, y, x, :, high], beside_y)
            copies.append((at_z, by_x, by_y))
        return copies

    def spread_two(buffer, copies):
        onward = []
        for at_z, by_x, by_y in copies:
            by_x.wait_recv()
            onward.append(same(buffer.at[at_z, y, :, :, low], beside_y))
            by_y.wait_recv()
            onward.append(same(buffer.at[at_z, :, x, :, high], beside_x))
        return onward

    token_z = along_z(rows)
    table_z = along_z(table)
    token_one = spread_one(rows, token_z)
    grad_z = along_z(grads)
    arrive(table_z)
    table_one = same(table.at[:, y, x], beside_x)
    token_two = spread_two(rows, token_one)
    table_one.wait_recv()
    table_two = same(table.at[:, y], beside_y)
    grad_one = spread_one(grads, grad_z)
    arrive(token_two)
    table_two.wait_recv()
    every = table[...].reshape(count, LANES)
    mine = lax.broadcasted_iota(jnp.int32, (count, LANES), 1) == me
    weight[...] = jnp.broadcast_to(
        jnp.sum(jnp.where(mine, every, 0.0), axis=1, keepdims=True), (count, LANES)
    )

    def project(buffer, matrix, first, target):
        def tile(step, carry):
            units = pl.ds(pl.multiple_of(first + step * TILE, TILE), TILE)
            columns = pl.ds(pl.multiple_of(step * TILE, TILE), TILE)
            target[:, columns] = contract_last(
                buffer[...].reshape(count, feat), matrix[units, :]
            )
            return carry

        lax.fori_loop(0, share // TILE, tile, 0)

    def partial(number, buffer, matrix):
        project(buffer, matrix, other_core * share, outgoing.at[number])
        return push(outgoing.at[number], theirs.at[number], beside_core)

    loads[0].wait()
    gate_sum = partial(0, rows, gate_w)
    loads[1].wait()
    up_sum = partial(1, rows, up_w)
    project(rows, gate_w, core * share, ours.at[0])
    grad_two = spread_two(grads, grad_one)
    project(rows, up_w, core * share, ours.at[1])
    loads[2].wait()
    arrive((gate_sum, up_sum))

    chunk = 2 * tok_count

    def activate(step, carry):
        part = pl.ds(pl.multiple_of(step * chunk, chunk), chunk)
        scale = weight[part, 0:1]
        up_value = ours[1, part, :] + theirs[1, part, :]
        activated, slope = silu_parts(ours[0, part, :] + theirs[0, part, :])
        hidden = activated * up_value
        whole_share[0, core, part, :] = hidden.astype(jnp.bfloat16)
        swapped[0, part, :] = (scale * hidden).astype(jnp.bfloat16)
        gate_by[part, :] = scale * up_value * slope
        up_by[part, :] = scale * activated
        return carry

    lax.fori_loop(0, count // chunk, activate, 0)
    hidden_share = same(whole_share.at[0, core], beside_core)
    trades = [push(swapped.at[0], swapped.at[1], opposite)]

    def combine(number, terms, scaled):
        def tile(step, carry):
            columns = pl.ds(pl.multiple_of(step * TILE, TILE), TILE)
            result = jnp.zeros((count, TILE), jnp.float32)
            for source, matrix in terms:
                for side in range(2):
                    result += jnp.dot(
                        whole_share[source, side],
                        matrix[side * share : (side + 1) * share, columns],
                        preferred_element_type=jnp.float32,
                    )
            if scaled:
                result = result * weight[:, 0:1]
            result = result.reshape(depth, 2, 2, tok_count, TILE)
            total[number, :, :, :, :, columns] = result
            lean[number, :, :, :, :, columns] = result.astype(jnp.bfloat16)
            return carry

        lax.fori_loop(0, feat // TILE, tile, 0)

    def reduce_one(number):
        return (
            push(lean.at[number, :, other_y, :, :, low], first_in.at[number, 0], beside_y),
            push(lean.at[number, :, :, other_x, :, high], first_in.at[number, 1], beside_x),
        )

    def reduce_two(number, copies):
        copies[0].wait_recv()
        second_out[number, 0] = (
            total[number, :, y, other_x, :, low]
            + first_in[number, 0, :, other_x].astype(jnp.float32)
        ).astype(jnp.bfloat16)
        onward = push(second_out.at[number, 0], second_in.at[number, 0], beside_x)
        copies[1].wait_recv()
        second_out[number, 1] = (
            total[number, :, other_y, x, :, high]
            + first_in[number, 1, :, other_y].astype(jnp.float32)
        ).astype(jnp.bfloat16)
        return onward, push(second_out.at[number, 1], second_in.at[number, 1], beside_y)

    def reduce_three(number, copies):
        arrive(copies)
        for side, (columns, index) in enumerate(((low, x), (high, y))):
            result = (
                total[number, :, y, x, :, columns]
                + first_in[number, side, :, index].astype(jnp.float32)
                + second_in[number, side].astype(jnp.float32)
            )
            last_own[number, :, :, columns] = result
            last_out[number, :, :, columns] = result.astype(jnp.bfloat16)
        return [
            push(
                last_out.at[number, lax.rem(z + step, depth)],
                last_in.at[number, step - 1],
                far[step - 1],
            )
            for step in range(1, depth)
        ]

    def reduce_end(number, copies, target):
        arrive(copies)
        result = last_own[number, z]
        for step in range(depth - 1):
            result += last_in[number, step].astype(jnp.float32)
        target[...] = result.astype(jnp.bfloat16)

    arrive(grad_two)
    grad_sum = partial(2, grads, down_w)
    project(grads, down_w, core * share, ours.at[2])
    grad_sum.wait_recv()

    def backward(step, carry):
        part = pl.ds(pl.multiple_of(step * chunk, chunk), chunk)
        hidden_grad = ours[2, part, :] + theirs[2, part, :]
        whole_share[1, core, part, :] = (hidden_grad * gate_by[part, :]).astype(jnp.bfloat16)
        whole_share[2, core, part, :] = (hidden_grad * up_by[part, :]).astype(jnp.bfloat16)
        return carry

    lax.fori_loop(0, count // chunk, backward, 0)
    gate_share = same(whole_share.at[1, core], beside_core)
    up_share = same(whole_share.at[2, core], beside_core)
    trades.append(push(whole_share.at[1, core], swapped.at[2], opposite))
    trades.append(push(whole_share.at[2, core], swapped.at[3], opposite))
    hidden_share.wait_recv()
    combine(0, ((0, down_w),), True)
    mixed_one = reduce_one(0)
    arrive((gate_share, up_share))
    combine(1, ((1, gate_w), (2, up_w)), False)
    back_one = reduce_one(1)
    mixed_two = reduce_two(0, mixed_one)
    mixed_three = reduce_three(0, mixed_two)
    back_two = reduce_two(1, back_one)
    back_three = reduce_three(1, back_two)

    flag = flags[0, me % (2 * depth)] == 1
    kept = []
    for number in range(3):
        trades[number].wait_recv()
        own = swapped[0] if number == 0 else whole_share[number, core]
        held[number, core] = jnp.where(flag, swapped[number + 1], own)
        kept.append(same(held.at[number, core], beside_core))
    reduce_end(0, mixed_three, mixed)
    reduce_end(1, back_three, input_grad)
    arrive(kept)
    for copy in sent:
        copy.wait_send()


def kernel_device(tokens, expert_ids, route_weight, swap_flags, w_gate, w_up, w_down, cotangent):
    tok_count, feat = tokens.shape
    depth = lax.axis_size("expert") // 4
    count = depth * 4 * tok_count
    units = w_gate.shape[1]
    share = units // 2
    half = feat // 2
    narrow, wide = jnp.bfloat16, jnp.float32
    grid = (depth, 2, 2, tok_count)
    vmem = pl.BlockSpec(memory_space=pltpu.VMEM)
    smem = pl.BlockSpec(memory_space=pltpu.SMEM)
    hbm = pl.BlockSpec(memory_space=pl.ANY)
    mixed, input_grad, rows, grads, held = pl.pallas_call(
        layer_kernel,
        out_shape=(
            jax.ShapeDtypeStruct((tok_count, feat), narrow),
            jax.ShapeDtypeStruct((tok_count, feat), narrow),
            jax.ShapeDtypeStruct(grid + (feat,), narrow),
            jax.ShapeDtypeStruct(grid + (feat,), narrow),
            jax.ShapeDtypeStruct((3, 2, count, share), narrow),
        ),
        in_specs=[vmem, vmem, vmem, smem, hbm, hbm, hbm, vmem],
        out_specs=(vmem,) * 5,
        scratch_shapes=[
            pltpu.VMEM((units, feat), narrow),
            pltpu.VMEM((units, feat), narrow),
            pltpu.VMEM((units, feat), narrow),
            pltpu.VMEM(grid + (LANES,), wide),
            pltpu.VMEM((count, LANES), wide),
            pltpu.VMEM((2,) + grid + (feat,), wide),
            pltpu.VMEM((2,) + grid + (feat,), narrow),
            pltpu.VMEM((3, count, share), wide),
            pltpu.VMEM((3, count, share), wide),
            pltpu.VMEM((3, count, share), wide),
            pltpu.VMEM((count, share), wide),
            pltpu.VMEM((count, share), wide),
            pltpu.VMEM((3, 2, count, share), narrow),
            pltpu.VMEM((4, count, share), narrow),
            pltpu.VMEM((2, 2, depth, 2, tok_count, half), narrow),
            pltpu.VMEM((2, 2, depth, tok_count, half), narrow),
            pltpu.VMEM((2, 2, depth, tok_count, half), narrow),
            pltpu.VMEM((2, depth, tok_count, feat), wide),
            pltpu.VMEM((2, depth, tok_count, feat), narrow),
            pltpu.VMEM((2, depth - 1, tok_count, feat), narrow),
            pltpu.SemaphoreType.DMA((3,)),
            pltpu.SemaphoreType.DMA((ROUTES,)),
            pltpu.SemaphoreType.DMA((ROUTES,)),
        ],
        compiler_params=pltpu.CompilerParams(
            collective_id=0, has_side_effects=True, vmem_limit_bytes=56 * 2**20
        ),
    )(
        tokens, expert_ids.T, route_weight.T, swap_flags[None], w_gate[0], w_up[0], w_down[0],
        cotangent,
    )
    rows, grads = rows.reshape(count, feat), grads.reshape(count, feat)
    tile = min(TILE, share)
    tiles = share // tile
    whole_rows = pl.BlockSpec((count, feat), lambda step: (0, 0))
    block = pl.BlockSpec((1, tile, feat), lambda step: (0, step, 0))
    gate, up, down = pl.pallas_call(
        outer_kernel,
        grid=(2 * tiles,),
        out_shape=(jax.ShapeDtypeStruct((1, units, feat), narrow),) * 3,
        in_specs=[
            pl.BlockSpec(
                (3, 1, count, tile), lambda step: (0, step // tiles, 0, lax.rem(step, tiles))
            ),
            whole_rows,
            whole_rows,
        ],
        out_specs=(block,) * 3,
        compiler_params=pltpu.CompilerParams(vmem_limit_bytes=56 * 2**20),
        cost_estimate=pl.CostEstimate(
            flops=6 * count * units * feat,
            bytes_accessed=6 * units * (feat + count) + 4 * count * feat,
            transcendentals=0,
        ),
    )(held, rows, grads)
    return mixed, input_grad, gate, up, down


def outer_kernel(held, rows, grads, gate, up, down):
    for number, other, target in ((1, rows, gate), (2, rows, up), (0, grads, down)):
        target[0] = contract_first(held[number, 0], other[...]).astype(jnp.bfloat16)


def per_device(*operands):
    experts, shards = lax.axis_size("expert"), lax.axis_size("dp")
    tok_count, feat = operands[0].shape
    units = operands[4].shape[1]
    fits = 8 <= experts <= 16 and experts % 8 == 0 and shards == 2 and tok_count % 16 == 0
    fits = fits and feat % TILE == 0 and units % (2 * TILE) == 0
    fits = fits and 3 * units * feat <= 6 * 2**20 and experts * tok_count <= 256
    return kernel_device(*operands) if fits else plain_device(*operands)


def solution(mesh):
    return jax.shard_map(
        per_device,
        mesh=mesh,
        in_specs=(
            P("expert", "dp"),
            P("expert", None),
            P("expert", None),
            P(),
            P("expert", None, "dp"),
            P("expert", None, "dp"),
            P("expert", None, "dp"),
            P("expert", "dp"),
        ),
        out_specs=(
            P("expert", "dp"),
            P("expert", "dp"),
            P("expert", None, "dp"),
            P("expert", None, "dp"),
            P("expert", None, "dp"),
        ),
        check_vma=False,
    )
```
